32 devices in a mesh: pole: 2 (over y), prow: 8 (over z, x), pcol: 2 (over core).
Axes of the slice: x: 2, y: 2, z: 4, core: 2. Of those that a mesh axis runs over, the one named last changes fastest.
Arguments:
- ancestor_inverse: float32 [2048, 1024], P(('pole', 'prow'), 'pcol'), parts along dimension 0, as said below
- pivots_one: float32 [8, 128, 128], P(('pole', 'pcol')), parts along dimension 0, may hold values from -6 to 6
- factor_one: float32 [2048, 512], P(('pole', 'prow'), 'pcol'), parts along dimension 0, may hold values from -0.25 to 0.25
- pattern_one: int32 [16, 4], P(('pole', 'prow')), parts along dimension 0, may hold values 0 or 1
- pivots_zero: float32 [16, 128, 128], P(('pole', 'pcol')), parts along dimension 0, may hold values from -6 to 6
- factor_zero: float32 [2048, 1024], P(('pole', 'prow'), 'pcol'), parts along dimension 0, may hold values from -0.375 to 0.375
- factor_parent: float32 [16, 128, 128], P(('pole', 'pcol')), parts along dimension 0, may hold values from -0.5 to 0.5
- parent_index: int32 [16], P(('pole', 'pcol')), parts along dimension 0, may hold values from 0 to 3
- pattern_zero: int32 [16, 8], P(('pole', 'prow'), 'pcol'), parts along dimension 0, may hold values 0 or 1
Outputs:
- cross_one: float32 [2048, 512], P(('pole', 'prow'), 'pcol'), parts along dimension 0
- diag_one: float32 [8, 128, 128], P(('pole', 'pcol')), parts along dimension 0
- cross_zero: float32 [2048, 1024], P(('pole', 'prow'), 'pcol'), parts along dimension 0
- parent_zero: float32 [16, 128, 128], P(('pole', 'pcol')), parts along dimension 0
- diag_zero: float32 [16, 128, 128], P(('pole', 'pcol')), parts along dimension 0
The draws below stay inside these ranges and needn't reach their ends.
There are 2 independent parts, one for each index of `pole`. The reference program is written for one: setup_inputs(seed, part) draws one part's arguments, and reference() takes and returns one part's arrays. A program takes and returns all parts, laid end to end along the dimension named above; each array names one. Nothing has to cross between parts.
Inputs may be any that keep to these rules, and one draw needn't show every extreme that they name: ancestor_inverse is symmetric up to rounding.
All inputs are finite; a program needn't handle non-finite values. No bound on the sum of `pattern_one` or of `pattern_zero` on one device may be relied on, other than what follows from the above.
Results may differ from the reference program's by a relative error of at most 0.000073.
Values sent between devices are 32-bit elements; how exact they have to be, the bound alone decides.
A program may use at most 128 MiB of HBM per device.

```python
import jax
import jax.numpy as jnp
from jax import lax

BLOCK = 128
ANC = 8
ONES = 4
ZEROS = 8


def draw_ancestor_inverse(key, part):
    key = jax.random.fold_in(key, 11)
    key_base = jax.random.fold_in(key, 0)
    order = ANC * BLOCK
    base = jax.random.normal(key_base, (order, order), jnp.float32)
    symmetric = (base + base.T) * 0.70710678
    return symmetric


def touch_ends(result, stream_key, smallest, high):
    longest = result.shape.index(max(result.shape))
    spots = []
    for shift in (0, 1):
        where = [jax.random.randint(jax.random.fold_in(stream_key, axis), (), 0, length) for axis, length in enumerate(result.shape)]
        where[longest] = (where[longest] + shift) % result.shape[longest]
        spots.append(tuple(where))
    return result.at[spots[0]].set(smallest).at[spots[1]].set(high)


def level_of(stream_key, dims, shards, low, top_value):
    loudness, own = 1.0, jax.random.fold_in(stream_key, 6)
    for axis_at, shards_of in shards:
        heights = jnp.exp(jax.random.uniform(jax.random.fold_in(own, axis_at), (shards_of,), jnp.float32, low / len(shards), top_value / len(shards)))
        loudness = loudness * jnp.repeat(heights, dims[axis_at] // shards_of).reshape([-1 if axis == axis_at else 1 for axis in range(len(dims))])
    return loudness


def normal_values(stream_key, dims, deviation, limit, cuts=(), held_as=jnp.bfloat16):
    entries = deviation * jax.random.normal(stream_key, dims, jnp.float32)
    if cuts:
        entries = entries * level_of(stream_key, dims, cuts, -0.22, 0.18)
    return jnp.clip(entries, -limit, limit).astype(held_as)


def setup_inputs(seed: int = 0, part: int = 0) -> dict:
    seeds = jax.random.split(jax.random.key(seed), 10)
    own_keys = jax.random.split(jax.random.fold_in(seeds[9], part), 10)
    ancestor_inverse = draw_ancestor_inverse(jax.random.fold_in(jax.random.fold_in(seeds[9], part), 71), part)
    pivots_one = normal_values(own_keys[1], (ONES, BLOCK, BLOCK), 1.0, 6.0, ((0, 2),), jnp.float32)
    factor_one = normal_values(own_keys[2], (ANC * BLOCK, ONES * BLOCK), (ANC * BLOCK // 2) ** -0.5, 0.25, ((0, 8), (1, 2)), jnp.float32)
    pattern_one = touch_ends((jax.random.randint(own_keys[3], (ANC, ONES), 0, 2) < 1).astype(jnp.int32), jax.random.fold_in(own_keys[3], 1), 0, 1)
    pivots_zero = normal_values(own_keys[4], (ZEROS, BLOCK, BLOCK), 1.0, 6.0, ((0, 2),), jnp.float32)
    factor_zero = normal_values(own_keys[5], (ANC * BLOCK, ZEROS * BLOCK), (ANC * BLOCK // 4) ** -0.5, 0.375, ((0, 8), (1, 2)), jnp.float32)
    factor_parent = normal_values(own_keys[6], (ZEROS, BLOCK, BLOCK), BLOCK ** -0.5, 0.5, ((0, 2),), jnp.float32)
    parent_index = touch_ends(jax.random.randint(own_keys[7], (ZEROS,), 0, ONES), jax.random.fold_in(own_keys[7], 1), 0, ONES - 1).astype(jnp.int32)
    pattern_zero = touch_ends((jax.random.randint(own_keys[8], (ANC, ZEROS), 0, 2) < 1).astype(jnp.int32), jax.random.fold_in(own_keys[8], 1), 0, 1)
    return {"ancestor_inverse": ancestor_inverse, "pivots_one": pivots_one, "factor_one": factor_one, "pattern_one": pattern_one, "pivots_zero": pivots_zero, "factor_zero": factor_zero, "factor_parent": factor_parent, "parent_index": parent_index, "pattern_zero": pattern_zero}


def expand_mask(pattern, width):
    return jnp.repeat(jnp.repeat(pattern.astype(jnp.float32), width, 0), width, 1)


def reference(ancestor_inverse, pivots_one, factor_one, pattern_one, pivots_zero, factor_zero, factor_parent, parent_index, pattern_zero):
    highest = lax.Precision.HIGHEST
    mask_one = expand_mask(pattern_one, BLOCK)
    level_one = factor_one * mask_one
    cross_full = -jnp.dot(ancestor_inverse, level_one, precision=highest, preferred_element_type=jnp.float32)
    shaped_one = level_one.reshape(ANC * BLOCK, ONES, BLOCK)
    cross_shaped = cross_full.reshape(ANC * BLOCK, ONES, BLOCK)
    diag_one = pivots_one - jnp.einsum("akb,akc->kbc", shaped_one, cross_shaped, precision=highest, preferred_element_type=jnp.float32)
    pattern_child = pattern_zero * jnp.take(pattern_one, parent_index, axis=1)
    mask_zero = expand_mask(pattern_child, BLOCK)
    level_zero = factor_zero * mask_zero
    shaped_zero = level_zero.reshape(ANC * BLOCK, ZEROS, BLOCK)
    parent_cols = jnp.take(cross_shaped, parent_index, axis=1)
    product = jnp.dot(ancestor_inverse, level_zero, precision=highest, preferred_element_type=jnp.float32)
    cross_child = -product.reshape(ANC * BLOCK, ZEROS, BLOCK) - jnp.einsum("acb,cbd->acd", parent_cols, factor_parent, precision=highest, preferred_element_type=jnp.float32)
    parents_inv = jnp.take(diag_one, parent_index, axis=0)
    parent_zero = -jnp.einsum("acb,acd->cbd", parent_cols, shaped_zero, precision=highest, preferred_element_type=jnp.float32) - jnp.einsum("cbe,ced->cbd", parents_inv, factor_parent, precision=highest, preferred_element_type=jnp.float32)
    diag_zero = pivots_zero - jnp.einsum("acb,acd->cbd", shaped_zero, cross_child, precision=highest, preferred_element_type=jnp.float32) - jnp.einsum("cba,cbd->cad", factor_parent, parent_zero, precision=highest, preferred_element_type=jnp.float32)
    cross_zero = cross_child.reshape(ANC * BLOCK, ZEROS * BLOCK) * mask_zero
    return (cross_full * mask_one, diag_one, cross_zero, parent_zero, diag_zero)
```

```python
import jax
import jax.numpy as jnp
from jax import lax
from jax.experimental import pallas as pl
from jax.experimental.pallas import tpu as pltpu
from jax.sharding import PartitionSpec as P


def expand_mask(pattern, width):
    return jnp.repeat(jnp.repeat(pattern, width, 0), width, 1)


def local(
    ancestor_inverse,
    pivots_one,
    factor_one,
    pattern_one,
    pivots_zero,
    factor_zero,
    factor_parent,
    parent_index,
    pattern_zero,
):
    highest = lax.Precision.HIGHEST
    band = lax.all_gather(ancestor_inverse, "pcol", axis=1, tiled=True)
    width = pivots_one.shape[1]
    rows = band.shape[0]
    one_local = pivots_one.shape[0]
    zero_local = pivots_zero.shape[0]
    column = lax.axis_index("pcol")
    total_one = one_local * lax.axis_size("pcol")
    pattern_float = pattern_one.astype(jnp.float32)
    own_pattern = lax.dynamic_slice_in_dim(pattern_float, column * one_local, one_local, 1)
    level_one = factor_one * expand_mask(own_pattern, width)
    selector = (parent_index[:, None] == jnp.arange(total_one, dtype=jnp.int32)[None, :]).astype(
        jnp.float32
    )
    parent_pattern = jnp.dot(
        pattern_float, selector.T, precision=highest, preferred_element_type=jnp.float32
    )
    child_pattern = pattern_zero.astype(jnp.float32) * parent_pattern
    child_mask = expand_mask(child_pattern, width)
    level_zero = factor_zero * child_mask

    def add_rows(piece):
        return jnp.dot(band, piece, precision=highest, preferred_element_type=jnp.float32)

    product_one = add_rows(lax.all_gather(level_one, "prow", axis=0, tiled=True))
    product_zero = add_rows(lax.all_gather(level_zero, "prow", axis=0, tiled=True))
    cross_full = -product_one
    shaped_one = level_one.reshape(rows, one_local, width)
    diag_partial = jnp.einsum(
        "akb,akc->kbc",
        shaped_one,
        cross_full.reshape(rows, one_local, width),
        precision=highest,
        preferred_element_type=jnp.float32,
    )
    diag_sum = lax.psum(diag_partial, "prow")
    diag_one = pivots_one - diag_sum
    cross_all, diag_all = (
        lax.all_gather(cross_full, "pcol", axis=1, tiled=True),
        lax.all_gather(diag_one, "pcol", axis=0, tiled=True),
    )
    parent_cols = jnp.einsum(
        "anb,cn->acb",
        cross_all.reshape(rows, total_one, width),
        selector,
        precision=highest,
        preferred_element_type=jnp.float32,
    )
    cross_child = -product_zero.reshape(rows, zero_local, width) - jnp.einsum(
        "acb,cbd->acd",
        parent_cols,
        factor_parent,
        precision=highest,
        preferred_element_type=jnp.float32,
    )
    shaped_zero = level_zero.reshape(rows, zero_local, width)
    parent_partial = jnp.einsum(
        "acb,acd->cbd",
        parent_cols,
        shaped_zero,
        precision=highest,
        preferred_element_type=jnp.float32,
    )
    child_partial = jnp.einsum(
        "acb,acd->cbd",
        shaped_zero,
        cross_child,
        precision=highest,
        preferred_element_type=jnp.float32,
    )
    parent_sum, child_sum = lax.psum((parent_partial, child_partial), "prow")
    parents_inv = jnp.einsum(
        "cn,nbd->cbd", selector, diag_all, precision=highest, preferred_element_type=jnp.float32
    )
    parent_zero = -parent_sum - jnp.einsum(
        "cbe,ced->cbd",
        parents_inv,
        factor_parent,
        precision=highest,
        preferred_element_type=jnp.float32,
    )
    diag_zero = (
        pivots_zero
        - child_sum
        - jnp.einsum(
            "cba,cbd->cad",
            factor_parent,
            parent_zero,
            precision=highest,
            preferred_element_type=jnp.float32,
        )
    )
    cross_one = cross_full * expand_mask(own_pattern, width)
    cross_zero = cross_child.reshape(rows, zero_local * width) * child_mask
    return (cross_one, diag_one, cross_zero, parent_zero, diag_zero)


RING = 8
OWN = 3
HALF = 5


def split(x):
    high = x.astype(jnp.bfloat16)
    return high, (x - high.astype(jnp.float32)).astype(jnp.bfloat16)


def dot3(a, b, dims=((1,), (0,))):
    def one(x, y):
        return lax.dot_general(x, y, (dims, ((), ())), preferred_element_type=jnp.float32)

    return one(a[0], b[0]) + (one(a[0], b[1]) + one(a[1], b[0]))


def natural(place):
    return 2 * place + (place // 4) * (15 - 4 * place)


def kernel(
    inverse, pivots_one, factor_one, pattern_one, pivots_zero, factor_zero, factor_parent, parent, pattern_zero,
    cross_one, diag_one, cross_zero, parent_zero, diag_zero,
    row, ones, ones_other, zeros, band, a_high, a_low, l_high, l_low, one_high, one_low, z, row_one, sums_one,
    ring_send, ring_recv, pair_send, pair_recv,
):
    w = pivots_one.shape[1]
    half_row = w // 2
    pole, prow, q = lax.axis_index("pole"), lax.axis_index("prow"), lax.axis_index("pcol")
    z_at, x_at = prow // 2, prow % 2
    place = z_at + x_at * (RING - 1 - 2 * z_at)
    right = (pole, natural((place + 1) % RING), q)
    left = (pole, natural((place + RING - 1) % RING), q)
    other = (pole, prow, 1 - q)

    barrier = pltpu.get_barrier_semaphore()
    for peer in (left, right, other):
        pl.semaphore_signal(barrier, inc=1, device_id=peer, device_id_type=pl.DeviceIdType.MESH)

    def block(k):
        return slice(k * w, (k + 1) * w)

    def flag(value):
        return value.astype(jnp.float32)

    mask_one = [flag(pattern_one[0, 2 * q + k]) for k in range(2)]
    parents = [parent[c] for c in range(4)]
    parent_mask = [sum(flag(p == k) * flag(pattern_one[0, k]) for k in range(4)) for p in parents]
    mask_zero = [flag(pattern_zero[0, c]) * parent_mask[c] for c in range(4)]
    for k in range(2):
        ones[OWN, :, block(k)] = factor_one[:, block(k)] * mask_one[k]
    for c in range(4):
        zeros[OWN, :, block(c)] = factor_zero[:, block(c)] * mask_zero[c]

    def copy(src, dst, send, recv, peer):
        return pltpu.make_async_remote_copy(
            src_ref=src, dst_ref=dst, send_sem=send, recv_sem=recv,
            device_id=peer, device_id_type=pl.DeviceIdType.MESH,
        )

    def to_ring(way, step, chunk):
        sign = -1 if way == 0 else 1
        source, target = OWN + sign * (step - 1), (OWN + sign * step) % RING
        ref = (ones, zeros, band)[chunk]
        src, dst = ref.at[source], ref.at[target]
        if chunk == 2:
            src, dst = ref.at[source, q], ref.at[target, q]
        place_at = (way, step - 1, chunk)
        return copy(src, dst, ring_send.at[place_at], ring_recv.at[place_at], right if way == 0 else left)

    def to_pair(kind, slot):
        if kind == 0:
            src, dst = ones.at[slot], ones_other.at[slot]
        elif kind == 1:
            src, dst = band.at[slot, q], band.at[slot, q]
        elif slot == 0:
            src, dst = inverse, row.at[q]
        elif slot == 1:
            src, dst = row_one.at[pl.ds(2 * q, 2)], row_one.at[pl.ds(2 * q, 2)]
        else:
            src, dst = sums_one.at[pl.ds(2 * q, 2)], sums_one.at[pl.ds(2 * q, 2)]
        return copy(src, dst, pair_send.at[kind, slot], pair_recv.at[kind, slot], other)

    started = []

    def start(made):
        made.start()
        started.append(made)

    pl.semaphore_wait(barrier, 3)
    start(to_pair(2, 0))
    for chunk in (0, 1):
        for way in (0, 1):
            start(to_ring(way, 1, chunk))
    start(to_pair(0, OWN))

    row[q] = inverse[...]
    to_pair(2, 0).wait_recv()
    for d in range(HALF):
        column = natural((place + d) % RING)
        source = (column // 4, slice(None), pl.ds(pl.multiple_of((column % 4) * w, w), w))
        piece = row[source]
        for h in range(2):
            band[OWN, h, :, block(d)] = piece[h * half_row : (h + 1) * half_row]
    for way in (0, 1):
        start(to_ring(way, 1, 2))

    def take_band(t):
        for d in range(HALF):
            piece = jnp.concatenate([band[t, h, :, block(d)] for h in range(2)], axis=0)
            u = (t + d) % RING
            a_high[block(t), block(u)], a_low[block(t), block(u)] = split(piece)
            if 0 < d < HALF - 1:
                a_high[block(u), block(t)], a_low[block(u), block(t)] = split(piece.T)

    def take_ones(t):
        high, low = split(ones[t])
        l_high[block(t), : 2 * w], l_low[block(t), : 2 * w] = high, low
        for k in range(2):
            one_high[2 * q + k, block(t), :] = high[:, block(k)]
            one_low[2 * q + k, block(t), :] = low[:, block(k)]

    def take_other(t):
        high, low = split(ones_other[t])
        for k in range(2):
            one_high[2 * (1 - q) + k, block(t), :] = high[:, block(k)]
            one_low[2 * (1 - q) + k, block(t), :] = low[:, block(k)]

    def take_zeros(t):
        l_high[block(t), 2 * w :], l_low[block(t), 2 * w :] = split(zeros[t])

    def times(rows, lo, hi):
        inner = slice(lo * w, hi * w)
        return dot3((a_high[rows, inner], a_low[rows, inner]), (l_high[inner, :], l_low[inner, :]))

    def add_old(lo, hi, new):
        @pl.loop(lo, hi)
        def _(t):
            rows = pl.ds(pl.multiple_of(t * w, w), w)
            total = z[rows, :]
            for n in new:
                total = total + times(rows, n, n + 1)
            z[rows, :] = total

    take_ones(OWN)
    take_zeros(OWN)
    take_band(OWN)
    z[block(OWN), :] = times(block(OWN), OWN, OWN + 1)

    for step in range(1, 4):
        last = step == 3
        for chunk in (0, 1, 2):
            for way in (0, 1):
                to_ring(way, step, chunk).wait_recv()
                t = OWN - step if way == 0 else OWN + step
                if not last or (chunk == 1) == (way == 0):
                    start(to_ring(way, step + 1, chunk))
                if chunk == 0:
                    start(to_pair(0, t))
                if chunk == 2:
                    start(to_pair(1, t))
        new = (OWN - step, OWN + step)
        if step == 1:
            to_pair(0, OWN).wait_recv()
            take_other(OWN)
        for t in new:
            take_ones(t)
            take_zeros(t)
            to_pair(0, t).wait_recv()
            take_other(t)
            to_pair(1, t).wait_recv()
            take_band(t)
        for t in new:
            z[block(t), :] = times(block(t), OWN - step, OWN + step + 1)
        add_old(OWN - step + 1, OWN + step, new)

    far = RING - 1
    to_ring(1, 4, 0).wait_recv()
    start(to_pair(0, far))
    take_ones(far)
    to_ring(1, 4, 2).wait_recv()
    start(to_pair(1, far))
    to_ring(0, 4, 1).wait_recv()
    take_zeros(far)
    to_pair(0, far).wait_recv()
    take_other(far)
    to_pair(1, far).wait_recv()
    take_band(far)
    add_old(0, far, (far,))
    z[block(far), :] = times(block(far), 0, RING)

    for k in range(2):
        row_one[2 * q + k] = z[block(OWN), block(k)]
    start(to_pair(2, 1))
    across = ((0,), (0,))
    for k in range(2):
        own = (l_high[:, block(k)], l_low[:, block(k)])
        made = pivots_one[k] + dot3(own, split(z[:, block(k)]), across)
        diag_one[k] = made
        sums_one[2 * q + k] = made
    start(to_pair(2, 2))
    for k in range(2):
        cross_one[:, block(k)] = -z[block(OWN), block(k)] * mask_one[k]

    for c in range(4):
        at = block(2 + c)
        product = split(z[:, at])
        p = parents[c]
        zeros_c = (l_high[:, at], l_low[:, at])
        parent_zero[c] = dot3((one_high[p], one_low[p]), product, across)
        diag_zero[c] = pivots_zero[c] + dot3(zeros_c, product, across)

    to_pair(2, 1).wait_recv()
    to_pair(2, 2).wait_recv()
    for c in range(4):
        p = parents[c]
        factor = split(factor_parent[c])
        lift = dot3(split(row_one[p]), factor)
        cross_zero[:, block(c)] = (lift - z[block(OWN), block(2 + c)]) * mask_zero[c]
        weight = parent_zero[c]
        sums = weight - dot3(split(sums_one[p]), factor)
        parent_zero[c] = sums
        diag_zero[c] = diag_zero[c] - dot3(split(weight), factor, across) - dot3(factor, split(sums), across)

    for made in started:
        made.wait_send()


def fused(*args):
    inverse, pivots_one, factor_one, _, pivots_zero, factor_zero, factor_parent, _, _ = args
    w = pivots_one.shape[1]
    rows = RING * w
    f32, b16 = jnp.float32, jnp.bfloat16
    vmem, smem = pl.BlockSpec(memory_space=pltpu.VMEM), pl.BlockSpec(memory_space=pltpu.SMEM)
    outs = (factor_one, pivots_one, factor_zero, factor_parent, pivots_zero)
    return pl.pallas_call(
        kernel,
        out_shape=tuple(jax.ShapeDtypeStruct(x.shape, f32) for x in outs),
        in_specs=[vmem, vmem, vmem, smem, vmem, vmem, vmem, smem, smem],
        out_specs=(vmem,) * 5,
        scratch_shapes=[
            pltpu.VMEM((2, w, 4 * w), f32),
            pltpu.VMEM((RING, w, 2 * w), f32),
            pltpu.VMEM((RING, w, 2 * w), f32),
            pltpu.VMEM((RING, w, 4 * w), f32),
            pltpu.VMEM((RING, 2, w // 2, HALF * w), f32),
            pltpu.VMEM((rows, rows), b16),
            pltpu.VMEM((rows, rows), b16),
            pltpu.VMEM((rows, 6 * w), b16),
            pltpu.VMEM((rows, 6 * w), b16),
            pltpu.VMEM((4, rows, w), b16),
            pltpu.VMEM((4, rows, w), b16),
            pltpu.VMEM((rows, 6 * w), f32),
            pltpu.VMEM((4, w, w), f32),
            pltpu.VMEM((4, w, w), f32),
            pltpu.SemaphoreType.DMA((2, 4, 3)),
            pltpu.SemaphoreType.DMA((2, 4, 3)),
            pltpu.SemaphoreType.DMA((3, RING)),
            pltpu.SemaphoreType.DMA((3, RING)),
        ],
        compiler_params=pltpu.CompilerParams(
            collective_id=0, has_side_effects=True, vmem_limit_bytes=48 * 1024 * 1024
        ),
    )(*args)


def solution(mesh):
    in_specs = (
        P(("pole", "prow"), "pcol"),
        P(("pole", "pcol"), None, None),
        P(("pole", "prow"), "pcol"),
        P(("pole", "prow"), None),
        P(("pole", "pcol"), None, None),
        P(("pole", "prow"), "pcol"),
        P(("pole", "pcol"), None, None),
        P(("pole", "pcol")),
        P(("pole", "prow"), "pcol"),
    )
    out_specs = (
        P(("pole", "prow"), "pcol"),
        P(("pole", "pcol"), None, None),
        P(("pole", "prow"), "pcol"),
        P(("pole", "pcol"), None, None),
        P(("pole", "pcol"), None, None),
    )
    ring = (mesh.shape["prow"], mesh.shape["pcol"]) == (RING, 2)
    return jax.shard_map(fused if ring else local, mesh=mesh, in_specs=in_specs, out_specs=out_specs, check_vma=False)
```

```python
import jax
import jax.numpy as jnp
from jax import lax
from jax.experimental import pallas as pl
from jax.experimental.pallas import tpu as pltpu
from jax.sharding import PartitionSpec as P


def expand_mask(pattern, width):
    return jnp.repeat(jnp.repeat(pattern, width, 0), width, 1)


def local(
    ancestor_inverse,
    pivots_one,
    factor_one,
    pattern_one,
    pivots_zero,
    factor_zero,
    factor_parent,
    parent_index,
    pattern_zero,
):
    highest = lax.Precision.HIGHEST
    band = lax.all_gather(ancestor_inverse, "pcol", axis=1, tiled=True)
    width = pivots_one.shape[1]
    rows = band.shape[0]
    one_local = pivots_one.shape[0]
    zero_local = pivots_zero.shape[0]
    column = lax.axis_index("pcol")
    total_one = one_local * lax.axis_size("pcol")
    pattern_float = pattern_one.astype(jnp.float32)
    own_pattern = lax.dynamic_slice_in_dim(pattern_float, column * one_local, one_local, 1)
    level_one = factor_one * expand_mask(own_pattern, width)
    selector = (parent_index[:, None] == jnp.arange(total_one, dtype=jnp.int32)[None, :]).astype(
        jnp.float32
    )
    parent_pattern = jnp.dot(
        pattern_float, selector.T, precision=highest, preferred_element_type=jnp.float32
    )
    child_pattern = pattern_zero.astype(jnp.float32) * parent_pattern
    child_mask = expand_mask(child_pattern, width)
    level_zero = factor_zero * child_mask

    def add_rows(piece):
        return jnp.dot(band, piece, precision=highest, preferred_element_type=jnp.float32)

    product_one = add_rows(lax.all_gather(level_one, "prow", axis=0, tiled=True))
    product_zero = add_rows(lax.all_gather(level_zero, "prow", axis=0, tiled=True))
    cross_full = -product_one
    shaped_one = level_one.reshape(rows, one_local, width)
    diag_partial = jnp.einsum(
        "akb,akc->kbc",
        shaped_one,
        cross_full.reshape(rows, one_local, width),
        precision=highest,
        preferred_element_type=jnp.float32,
    )
    diag_sum = lax.psum(diag_partial, "prow")
    diag_one = pivots_one - diag_sum
    cross_all, diag_all = (
        lax.all_gather(cross_full, "pcol", axis=1, tiled=True),
        lax.all_gather(diag_one, "pcol", axis=0, tiled=True),
    )
    parent_cols = jnp.einsum(
        "anb,cn->acb",
        cross_all.reshape(rows, total_one, width),
        selector,
        precision=highest,
        preferred_element_type=jnp.float32,
    )
    cross_child = -product_zero.reshape(rows, zero_local, width) - jnp.einsum(
        "acb,cbd->acd",
        parent_cols,
        factor_parent,
        precision=highest,
        preferred_element_type=jnp.float32,
    )
    shaped_zero = level_zero.reshape(rows, zero_local, width)
    parent_partial = jnp.einsum(
        "acb,acd->cbd",
        parent_cols,
        shaped_zero,
        precision=highest,
        preferred_element_type=jnp.float32,
    )
    child_partial = jnp.einsum(
        "acb,acd->cbd",
        shaped_zero,
        cross_child,
        precision=highest,
        preferred_element_type=jnp.float32,
    )
    parent_sum, child_sum = lax.psum((parent_partial, child_partial), "prow")
    parents_inv = jnp.einsum(
        "cn,nbd->cbd", selector, diag_all, precision=highest, preferred_element_type=jnp.float32
    )
    parent_zero = -parent_sum - jnp.einsum(
        "cbe,ced->cbd",
        parents_inv,
        factor_parent,
        precision=highest,
        preferred_element_type=jnp.float32,
    )
    diag_zero = (
        pivots_zero
        - child_sum
        - jnp.einsum(
            "cba,cbd->cad",
            factor_parent,
            parent_zero,
            precision=highest,
            preferred_element_type=jnp.float32,
        )
    )
    cross_one = cross_full * expand_mask(own_pattern, width)
    cross_zero = cross_child.reshape(rows, zero_local * width) * child_mask
    return (cross_one, diag_one, cross_zero, parent_zero, diag_zero)


VMEM_BYTES = 64 * 1024 * 1024
RING = 8
OWN = 3
HALF = 5


def split(x):
    high = x.astype(jnp.bfloat16)
    return high, (x - high.astype(jnp.float32)).astype(jnp.bfloat16)


def dot3(a, b, dims=((1,), (0,))):
    def one(x, y):
        return lax.dot_general(x, y, (dims, ((), ())), preferred_element_type=jnp.float32)

    return one(a[0], b[0]) + (one(a[0], b[1]) + one(a[1], b[0]))


def natural(place):
    return 2 * place + (place // 4) * (15 - 4 * place)


def kernel(
    inverse, pivots_one_hbm, factor_one_hbm, pattern_one, pivots_zero_hbm, factor_zero_hbm, factor_parent_hbm,
    parent, pattern_zero, cross_one_hbm, diag_one_hbm, cross_zero_hbm, parent_zero_hbm, diag_zero_hbm,
    cross_one, diag_one, cross_zero, parent_zero, diag_zero, pivots_one, factor_one, pivots_zero, factor_zero, factor_parent, row, ones, ones_other, zeros, band, a_high, a_low, l_high, l_low, one_high, one_low,
    z, u, u_high, u_low, half_one, half_zero, mixed, row_one, sums_one,
    ring_send, ring_recv, pair_send, pair_recv, load_done, store_done,
):
    w = pivots_zero.shape[1]
    half_row = w // 2
    pole, prow, q = lax.axis_index("pole"), lax.axis_index("prow"), lax.axis_index("pcol")
    z_at, x_at = prow // 2, prow % 2
    place = z_at + x_at * (RING - 1 - 2 * z_at)
    right = (pole, natural((place + 1) % RING), q)
    left = (pole, natural((place + RING - 1) % RING), q)
    other = (pole, prow, 1 - q)

    barrier = pltpu.get_barrier_semaphore()
    for peer in (left, right, other):
        pl.semaphore_signal(barrier, inc=1, device_id=peer, device_id_type=pl.DeviceIdType.MESH)

    loads = [
        pltpu.make_async_copy(src, dst, load_done.at[n])
        for n, (src, dst) in enumerate(
            (
                (factor_one_hbm, factor_one),
                (factor_zero_hbm, factor_zero),
                (inverse, row.at[q]),
                (pivots_one_hbm, pivots_one.at[pl.ds(2 * q, 2)]),
                (pivots_zero_hbm, pivots_zero),
                (factor_parent_hbm, factor_parent),
            )
        )
    ]
    for load in loads:
        load.start()

    def block(k):
        return slice(k * w, (k + 1) * w)

    def flag(value):
        return value.astype(jnp.float32)

    mask_one = [flag(pattern_one[0, 2 * q + k]) for k in range(2)]
    parents = [parent[c] for c in range(4)]
    parent_mask = [sum(flag(p == k) * flag(pattern_one[0, k]) for k in range(4)) for p in parents]
    mask_zero = [flag(pattern_zero[0, c]) * parent_mask[c] for c in range(4)]
    loads[0].wait()
    for k in range(2):
        ones[OWN, :, block(k)] = factor_one[:, block(k)] * mask_one[k]
    loads[1].wait()
    for c in range(4):
        zeros[OWN, :, block(c)] = factor_zero[:, block(c)] * mask_zero[c]

    def copy(src, dst, send, recv, peer):
        return pltpu.make_async_remote_copy(
            src_ref=src, dst_ref=dst, send_sem=send, recv_sem=recv,
            device_id=peer, device_id_type=pl.DeviceIdType.MESH,
        )

    def to_ring(way, step, chunk):
        sign = -1 if way == 0 else 1
        source, target = OWN + sign * (step - 1), (OWN + sign * step) % RING
        ref = (ones, zeros, band)[chunk]
        src, dst = ref.at[source], ref.at[target]
        if chunk == 2:
            src, dst = ref.at[source, q], ref.at[target, q]
        place_at = (way, step - 1, chunk)
        return copy(src, dst, ring_send.at[place_at], ring_recv.at[place_at], right if way == 0 else left)

    def to_pair(kind, slot):
        if kind == 0:
            src, dst = ones.at[slot], ones_other.at[slot]
        elif kind == 1:
            src, dst = band.at[slot, q], band.at[slot, q]
        elif slot == 0:
            src, dst = inverse, row.at[q]
        else:
            src, dst = pivots_one_hbm, pivots_one.at[pl.ds(2 * q, 2)]
        return copy(src, dst, pair_send.at[kind, slot], pair_recv.at[kind, slot], other)

    stores = [
        pltpu.make_async_copy(src, dst, store_done.at[n])
        for n, (src, dst) in enumerate(
            (
                (cross_one, cross_one_hbm),
                (diag_one, diag_one_hbm),
                (cross_zero, cross_zero_hbm),
                (parent_zero, parent_zero_hbm),
                (diag_zero, diag_zero_hbm),
            )
        )
    ]
    started = []

    def start(made):
        made.start()
        started.append(made)

    pl.semaphore_wait(barrier, 3)
    start(to_pair(2, 0))
    for chunk in (0, 1):
        for way in (0, 1):
            start(to_ring(way, 1, chunk))
    start(to_pair(0, OWN))
    start(to_pair(2, 1))

    loads[2].wait()
    to_pair(2, 0).wait_recv()
    for d in range(HALF):
        column = natural((place + d) % RING)
        source = (column // 4, slice(None), pl.ds(pl.multiple_of((column % 4) * w, w), w))
        piece = row[source]
        for h in range(2):
            band[OWN, h, :, block(d)] = piece[h * half_row : (h + 1) * half_row]
    for way in (0, 1):
        start(to_ring(way, 1, 2))

    def take_band(t):
        for d in range(HALF):
            piece = jnp.concatenate([band[t, h, :, block(d)] for h in range(2)], axis=0)
            u = (t + d) % RING
            a_high[block(t), block(u)], a_low[block(t), block(u)] = split(piece)
            if 0 < d < HALF - 1:
                a_high[block(u), block(t)], a_low[block(u), block(t)] = split(piece.T)

    def take_half(t, blocks, column):
        high, low = split(blocks[t])
        lanes = pl.ds(pl.multiple_of(2 * column * w, 2 * w), 2 * w)
        l_high[block(t), lanes], l_low[block(t), lanes] = high, low
        for k in range(2):
            one_high[2 * column + k, block(t), :] = high[:, block(k)]
            one_low[2 * column + k, block(t), :] = low[:, block(k)]

    def take_ones(t):
        take_half(t, ones, q)

    def take_other(t):
        take_half(t, ones_other, 1 - q)

    def take_zeros(t):
        l_high[block(t), 4 * w :], l_low[block(t), 4 * w :] = split(zeros[t])

    def times(n, lo, hi):
        inner = slice(lo * w, hi * w)
        return dot3((a_high[block(n), inner], a_low[block(n), inner]), (l_high[inner, :], l_low[inner, :]))

    across = ((0,), (0,))

    def put(ref, k, value, first):
        ref[k] = value if first else ref[k] + value

    def absorb(n, lo, hi):
        first = lo == hi
        z[...] = times(n, n, n + 1)
        if first:
            for k in range(4):
                row_one[k] = z[:, block(k)]
            cross_zero[...] = z[:, 4 * w :]
        else:
            u[...] = times(n, lo, hi)
            new = times(OWN, n, n + 1)
            for k in range(4):
                row_one[k] = row_one[k] + new[:, block(k)]
                u_high[k], u_low[k] = split(u[:, block(k)])
            cross_zero[...] = cross_zero[...] + new[:, 4 * w :]

        def part(k, weight):
            own = weight * z[:, block(k)]
            return split(own if first else own + u[:, block(k)])

        for k in range(8):
            sums = dot3((l_high[block(n), block(k)], l_low[block(n), block(k)]), part(k, 0.5), across)
            put(half_one if k < 4 else half_zero, k % 4, sums, first)
        for c in range(4):
            p = parents[c]
            left_side = (one_high[p, block(n), :], one_low[p, block(n), :])
            right_side = part(4 + c, 1.0)
            if not first:
                zeros_c = (l_high[block(n), block(4 + c)], l_low[block(n), block(4 + c)])
                left_side = [jnp.concatenate(x, axis=0) for x in zip(left_side, (u_high[p], u_low[p]))]
                right_side = [jnp.concatenate(x, axis=0) for x in zip(right_side, zeros_c)]
            put(mixed, c, dot3(left_side, right_side, across), first)

    take_ones(OWN)
    take_zeros(OWN)
    take_band(OWN)
    to_pair(0, OWN).wait_recv()
    take_other(OWN)
    absorb(OWN, OWN, OWN)

    for step in range(1, 4):
        last = step == 3
        for chunk in (0, 1, 2):
            for way in (0, 1):
                to_ring(way, step, chunk).wait_recv()
                t = OWN - step if way == 0 else OWN + step
                if not last or (chunk == 1) == (way == 0):
                    start(to_ring(way, step + 1, chunk))
                if chunk == 0:
                    start(to_pair(0, t))
                if chunk == 2:
                    start(to_pair(1, t))
        new = (OWN - step, OWN + step)
        for t in new:
            take_ones(t)
            take_zeros(t)
            to_pair(0, t).wait_recv()
            take_other(t)
            to_pair(1, t).wait_recv()
            take_band(t)
        absorb(OWN - step, OWN - step + 1, OWN + step)
        absorb(OWN + step, OWN - step, OWN + step)

    far = RING - 1
    to_ring(1, 4, 0).wait_recv()
    start(to_pair(0, far))
    take_ones(far)
    to_ring(1, 4, 2).wait_recv()
    start(to_pair(1, far))
    to_ring(0, 4, 1).wait_recv()
    take_zeros(far)
    to_pair(0, far).wait_recv()
    take_other(far)
    to_pair(1, far).wait_recv()
    take_band(far)
    for load in loads[3:]:
        load.wait()
    to_pair(2, 1).wait_recv()
    absorb(far, 0, far)

    for k in range(4):
        sums_one[k] = pivots_one[k] + half_one[k] + half_one[k].T
    for k in range(2):
        diag_one[k] = sums_one[2 * q + k]
        cross_one[:, block(k)] = -row_one[2 * q + k] * mask_one[k]
    stores[0].start()
    stores[1].start()
    for c in range(4):
        p = parents[c]
        factor = split(factor_parent[c])
        weight = mixed[c]
        lift = dot3(split(row_one[p]), factor)
        cross_zero[:, block(c)] = (lift - cross_zero[:, block(c)]) * mask_zero[c]
        sums = weight - dot3(split(sums_one[p]), factor)
        parent_zero[c] = sums
        own = pivots_zero[c] + half_zero[c] + half_zero[c].T
        diag_zero[c] = own - dot3(split(weight), factor, across) - dot3(factor, split(sums), across)
    for store_out in stores[2:]:
        store_out.start()
    for made in started:
        made.wait_send()
    for store_out in stores:
        store_out.wait()


def store(*refs):
    ins, outs, held, (load_done, store_done) = refs[:5], refs[5:10], refs[10:15], refs[15:]
    loads = [pltpu.make_async_copy(ins[n], held[n], load_done.at[n]) for n in range(5)]
    stores = [pltpu.make_async_copy(held[n], outs[n], store_done.at[n]) for n in range(5)]
    for load in loads:
        load.start()
    for load, out in zip(loads, stores):
        load.wait()
        out.start()
    for out in stores:
        out.wait()


def fused(*args):
    inverse, pivots_one, factor_one, _, pivots_zero, factor_zero, factor_parent, _, _ = args
    w = pivots_one.shape[1]
    rows = RING * w
    f32, b16 = jnp.float32, jnp.bfloat16
    vmem, smem = pl.BlockSpec(memory_space=pltpu.VMEM), pl.BlockSpec(memory_space=pltpu.SMEM)
    hbm = pl.BlockSpec(memory_space=pltpu.HBM)
    outs = (factor_one, pivots_one, factor_zero, factor_parent, pivots_zero)
    made = pl.pallas_call(
        kernel,
        out_shape=tuple(jax.ShapeDtypeStruct(x.shape, f32) for x in outs),
        in_specs=[hbm, hbm, hbm, smem, hbm, hbm, hbm, smem, smem],
        out_specs=(hbm,) * 5,
        scratch_shapes=[
            *(pltpu.VMEM(x.shape, f32) for x in outs),
            pltpu.VMEM((4, w, w), f32),
            *(pltpu.VMEM(x.shape, f32) for x in (factor_one, pivots_zero, factor_zero, factor_parent)),
            pltpu.VMEM((2, w, 4 * w), f32),
            pltpu.VMEM((RING, w, 2 * w), f32),
            pltpu.VMEM((RING, w, 2 * w), f32),
            pltpu.VMEM((RING, w, 4 * w), f32),
            pltpu.VMEM((RING, 2, w // 2, HALF * w), f32),
            pltpu.VMEM((rows, rows), b16),
            pltpu.VMEM((rows, rows), b16),
            pltpu.VMEM((rows, 8 * w), b16),
            pltpu.VMEM((rows, 8 * w), b16),
            pltpu.VMEM((4, rows, w), b16),
            pltpu.VMEM((4, rows, w), b16),
            pltpu.VMEM((w, 8 * w), f32),
            pltpu.VMEM((w, 8 * w), f32),
            pltpu.VMEM((4, w, w), b16),
            pltpu.VMEM((4, w, w), b16),
            *(pltpu.VMEM((4, w, w), f32) for _ in range(5)),
            pltpu.SemaphoreType.DMA((2, 4, 3)),
            pltpu.SemaphoreType.DMA((2, 4, 3)),
            pltpu.SemaphoreType.DMA((3, RING)),
            pltpu.SemaphoreType.DMA((3, RING)),
            pltpu.SemaphoreType.DMA((6,)),
            pltpu.SemaphoreType.DMA((5,)),
        ],
        compiler_params=pltpu.CompilerParams(
            collective_id=0, has_side_effects=True, vmem_limit_bytes=VMEM_BYTES
        ),
    )(*args)
    return pl.pallas_call(
        store,
        out_shape=tuple(jax.ShapeDtypeStruct(x.shape, f32) for x in outs),
        in_specs=[hbm] * 5,
        out_specs=(hbm,) * 5,
        scratch_shapes=[
            *(pltpu.VMEM(x.shape, f32) for x in outs),
            pltpu.SemaphoreType.DMA((5,)),
            pltpu.SemaphoreType.DMA((5,)),
        ],
        compiler_params=pltpu.CompilerParams(vmem_limit_bytes=VMEM_BYTES),
    )(*made)


def solution(mesh):
    in_specs = (
        P(("pole", "prow"), "pcol"),
        P(("pole", "pcol"), None, None),
        P(("pole", "prow"), "pcol"),
        P(("pole", "prow"), None),
        P(("pole", "pcol"), None, None),
        P(("pole", "prow"), "pcol"),
        P(("pole", "pcol"), None, None),
        P(("pole", "pcol")),
        P(("pole", "prow"), "pcol"),
    )
    out_specs = (
        P(("pole", "prow"), "pcol"),
        P(("pole", "pcol"), None, None),
        P(("pole", "prow"), "pcol"),
        P(("pole", "pcol"), None, None),
        P(("pole", "pcol"), None, None),
    )
    ring = (mesh.shape["prow"], mesh.shape["pcol"]) == (RING, 2)
    return jax.shard_map(fused if ring else local, mesh=mesh, in_specs=in_specs, out_specs=out_specs, check_vma=False)
```

```python
import jax
import jax.numpy as jnp
from jax import lax
from jax.experimental import pallas as pl
from jax.experimental.pallas import tpu as pltpu
from jax.sharding import PartitionSpec as P


def expand_mask(pattern, width):
    return jnp.repeat(jnp.repeat(pattern, width, 0), width, 1)


def local(
    ancestor_inverse,
    pivots_one,
    factor_one,
    pattern_one,
    pivots_zero,
    factor_zero,
    factor_parent,
    parent_index,
    pattern_zero,
):
    highest = lax.Precision.HIGHEST
    band = lax.all_gather(ancestor_inverse, "pcol", axis=1, tiled=True)
    width = pivots_one.shape[1]
    rows = band.shape[0]
    one_local = pivots_one.shape[0]
    zero_local = pivots_zero.shape[0]
    column = lax.axis_index("pcol")
    total_one = one_local * lax.axis_size("pcol")
    pattern_float = pattern_one.astype(jnp.float32)
    own_pattern = lax.dynamic_slice_in_dim(pattern_float, column * one_local, one_local, 1)
    level_one = factor_one * expand_mask(own_pattern, width)
    selector = (parent_index[:, None] == jnp.arange(total_one, dtype=jnp.int32)[None, :]).astype(
        jnp.float32
    )
    parent_pattern = jnp.dot(
        pattern_float, selector.T, precision=highest, preferred_element_type=jnp.float32
    )
    child_pattern = pattern_zero.astype(jnp.float32) * parent_pattern
    child_mask = expand_mask(child_pattern, width)
    level_zero = factor_zero * child_mask

    def add_rows(piece):
        return jnp.dot(band, piece, precision=highest, preferred_element_type=jnp.float32)

    product_one = add_rows(lax.all_gather(level_one, "prow", axis=0, tiled=True))
    product_zero = add_rows(lax.all_gather(level_zero, "prow", axis=0, tiled=True))
    cross_full = -product_one
    shaped_one = level_one.reshape(rows, one_local, width)
    diag_partial = jnp.einsum(
        "akb,akc->kbc",
        shaped_one,
        cross_full.reshape(rows, one_local, width),
        precision=highest,
        preferred_element_type=jnp.float32,
    )
    diag_sum = lax.psum(diag_partial, "prow")
    diag_one = pivots_one - diag_sum
    cross_all, diag_all = (
        lax.all_gather(cross_full, "pcol", axis=1, tiled=True),
        lax.all_gather(diag_one, "pcol", axis=0, tiled=True),
    )
    parent_cols = jnp.einsum(
        "anb,cn->acb",
        cross_all.reshape(rows, total_one, width),
        selector,
        precision=highest,
        preferred_element_type=jnp.float32,
    )
    cross_child = -product_zero.reshape(rows, zero_local, width) - jnp.einsum(
        "acb,cbd->acd",
        parent_cols,
        factor_parent,
        precision=highest,
        preferred_element_type=jnp.float32,
    )
    shaped_zero = level_zero.reshape(rows, zero_local, width)
    parent_partial = jnp.einsum(
        "acb,acd->cbd",
        parent_cols,
        shaped_zero,
        precision=highest,
        preferred_element_type=jnp.float32,
    )
    child_partial = jnp.einsum(
        "acb,acd->cbd",
        shaped_zero,
        cross_child,
        precision=highest,
        preferred_element_type=jnp.float32,
    )
    parent_sum, child_sum = lax.psum((parent_partial, child_partial), "prow")
    parents_inv = jnp.einsum(
        "cn,nbd->cbd", selector, diag_all, precision=highest, preferred_element_type=jnp.float32
    )
    parent_zero = -parent_sum - jnp.einsum(
        "cbe,ced->cbd",
        parents_inv,
        factor_parent,
        precision=highest,
        preferred_element_type=jnp.float32,
    )
    diag_zero = (
        pivots_zero
        - child_sum
        - jnp.einsum(
            "cba,cbd->cad",
            factor_parent,
            parent_zero,
            precision=highest,
            preferred_element_type=jnp.float32,
        )
    )
    cross_one = cross_full * expand_mask(own_pattern, width)
    cross_zero = cross_child.reshape(rows, zero_local * width) * child_mask
    return (cross_one, diag_one, cross_zero, parent_zero, diag_zero)


VMEM_BYTES = 64 * 1024 * 1024
RING = 8
OWN = 3
HALF = 5


def split(x):
    high = x.astype(jnp.bfloat16)
    return high, (x - high.astype(jnp.float32)).astype(jnp.bfloat16)


def dot3(a, b, dims=((1,), (0,))):
    def one(x, y):
        return lax.dot_general(x, y, (dims, ((), ())), preferred_element_type=jnp.float32)

    return one(a[0], b[0]) + (one(a[0], b[1]) + one(a[1], b[0]))


def natural(place):
    return 2 * place + (place // 4) * (15 - 4 * place)


def kernel(
    inverse, pivots_one_hbm, factor_one_hbm, pattern_one, pivots_zero_hbm, factor_zero_hbm, factor_parent_hbm,
    parent, pattern_zero, cross_one_hbm, diag_one_hbm, cross_zero_hbm, parent_zero_hbm, diag_zero_hbm,
    cross_one, diag_one, cross_zero, parent_zero, diag_zero, pivots_one, factor_one, pivots_zero, factor_zero, factor_parent, row, ones, ones_other, zeros, band, a_high, a_low, l_high, l_low, one_high, one_low,
    z, u, u_high, u_low, half_one, half_zero, mixed, row_one, sums_one,
    ring_send, ring_recv, pair_send, pair_recv, load_done, store_done,
):
    w = pivots_zero.shape[1]
    half_row, eighth = w // 2, w // 16
    pole, prow, q = lax.axis_index("pole"), lax.axis_index("prow"), lax.axis_index("pcol")
    z_at, x_at = prow // 2, prow % 2
    place = z_at + x_at * (RING - 1 - 2 * z_at)
    right = (pole, natural((place + 1) % RING), q)
    left = (pole, natural((place + RING - 1) % RING), q)
    other = (pole, prow, 1 - q)

    barrier = pltpu.get_barrier_semaphore()
    for peer in (left, right, other):
        pl.semaphore_signal(barrier, inc=1, device_id=peer, device_id_type=pl.DeviceIdType.MESH)

    loads = [
        pltpu.make_async_copy(src, dst, load_done.at[n])
        for n, (src, dst) in enumerate(
            (
                (factor_one_hbm, factor_one),
                (factor_zero_hbm, factor_zero),
                (inverse, row.at[q]),
                (pivots_one_hbm, pivots_one.at[pl.ds(2 * q, 2)]),
                (pivots_zero_hbm, pivots_zero),
                (factor_parent_hbm, factor_parent),
            )
        )
    ]
    for load in loads:
        load.start()

    def block(k):
        return slice(k * w, (k + 1) * w)

    def flag(value):
        return value.astype(jnp.float32)

    mask_one = [flag(pattern_one[0, 2 * q + k]) for k in range(2)]
    parents = [parent[c] for c in range(4)]
    parent_mask = [sum(flag(p == k) * flag(pattern_one[0, k]) for k in range(4)) for p in parents]
    mask_zero = [flag(pattern_zero[0, c]) * parent_mask[c] for c in range(4)]
    loads[0].wait()
    for k in range(2):
        ones[OWN, :, block(k)] = factor_one[:, block(k)] * mask_one[k]
    loads[1].wait()
    for c in range(4):
        zeros[OWN, :, block(c)] = factor_zero[:, block(c)] * mask_zero[c]

    def copy(src, dst, send, recv, peer):
        return pltpu.make_async_remote_copy(
            src_ref=src, dst_ref=dst, send_sem=send, recv_sem=recv,
            device_id=peer, device_id_type=pl.DeviceIdType.MESH,
        )

    def to_ring(way, step, chunk):
        sign = -1 if way == 0 else 1
        source, target = OWN + sign * (step - 1), (OWN + sign * step) % RING
        ref = (ones, zeros, band)[chunk]
        src, dst = ref.at[source], ref.at[target]
        if chunk == 2:
            src, dst = ref.at[source, q], ref.at[target, q]
        place_at = (way, step - 1, chunk)
        return copy(src, dst, ring_send.at[place_at], ring_recv.at[place_at], right if way == 0 else left)

    def to_pair(kind, slot):
        if kind == 0:
            src, dst = ones.at[slot], ones_other.at[slot]
        elif kind == 1:
            src, dst = band.at[slot, q], band.at[slot, q]
        elif slot == 0:
            src, dst = inverse, row.at[q]
        else:
            src, dst = pivots_one_hbm, pivots_one.at[pl.ds(2 * q, 2)]
        return copy(src, dst, pair_send.at[kind, slot], pair_recv.at[kind, slot], other)

    stores = [
        pltpu.make_async_copy(src, dst, store_done.at[n])
        for n, (src, dst) in enumerate(
            (
                (cross_one, cross_one_hbm),
                (diag_one, diag_one_hbm),
                (cross_zero, cross_zero_hbm),
                (parent_zero, parent_zero_hbm),
                (diag_zero, diag_zero_hbm),
            )
        )
    ]
    started = []

    def start(made):
        made.start()
        started.append(made)

    pl.semaphore_wait(barrier, 3)
    start(to_pair(2, 0))
    for way in (0, 1):
        start(to_ring(way, 1, 0))
    start(to_pair(0, OWN))
    start(to_pair(2, 1))

    loads[2].wait()
    to_pair(2, 0).wait_recv()
    for d in range(HALF):
        column = natural((place + d) % RING)
        source = (column // 4, slice(None), pl.ds(pl.multiple_of((column % 4) * w, w), w))
        piece = row[source]
        for h in range(2):
            if d < HALF - 1:
                band[OWN, h, :half_row, block(d)] = piece[h * half_row : (h + 1) * half_row]
            else:
                sent = jnp.where(place < RING // 2, piece[:half_row], piece.T[half_row:])
                for n in range(4):
                    at = (4 * h + n) * eighth
                    band[OWN, h, half_row:, block(n)] = sent[at : at + eighth]
    for chunk in (2, 1):
        for way in (0, 1):
            start(to_ring(way, 1, chunk))

    def take_band(t):
        for d in range(HALF - 1):
            piece = jnp.concatenate([band[t, h, :half_row, block(d)] for h in range(2)], axis=0)
            u = (t + d) % RING
            a_high[block(t), block(u)], a_low[block(t), block(u)] = split(piece)
            if d > 0:
                a_high[block(u), block(t)], a_low[block(u), block(t)] = split(piece.T)

    def take_pair(t):
        u = t + RING // 2
        low = (place + t + RING - OWN) % RING < RING // 2
        at_t, at_u = (
            jnp.concatenate([band[v, h, half_row:, block(n)] for h in range(2) for n in range(4)], axis=0)
            for v in (t, u)
        )
        piece = jnp.concatenate([jnp.where(low, at_t, at_u), jnp.where(low, at_u, at_t)], axis=0)
        turned = piece.T
        a_high[block(t), block(u)], a_low[block(t), block(u)] = split(jnp.where(low, piece, turned))
        a_high[block(u), block(t)], a_low[block(u), block(t)] = split(jnp.where(low, turned, piece))

    def take_half(t, blocks, column):
        high, low = split(blocks[t])
        lanes = pl.ds(pl.multiple_of(2 * column * w, 2 * w), 2 * w)
        l_high[block(t), lanes], l_low[block(t), lanes] = high, low
        for k in range(2):
            one_high[2 * column + k, block(t), :] = high[:, block(k)]
            one_low[2 * column + k, block(t), :] = low[:, block(k)]

    def take_ones(t):
        take_half(t, ones, q)

    def take_other(t):
        take_half(t, ones_other, 1 - q)

    def take_zeros(t):
        l_high[block(t), 4 * w :], l_low[block(t), 4 * w :] = split(zeros[t])

    def times(n, lo, hi):
        inner = slice(lo * w, hi * w)
        return dot3((a_high[block(n), inner], a_low[block(n), inner]), (l_high[inner, :], l_low[inner, :]))

    across = ((0,), (0,))

    def put(ref, k, value, first):
        ref[k] = value if first else ref[k] + value

    def absorb(n, lo, hi):
        first = lo == hi
        z[...] = times(n, n, n + 1)
        if first:
            for k in range(4):
                row_one[k] = z[:, block(k)]
            cross_zero[...] = z[:, 4 * w :]
        else:
            u[...] = times(n, lo, hi)
            new = times(OWN, n, n + 1)
            for k in range(4):
                row_one[k] = row_one[k] + new[:, block(k)]
                u_high[k], u_low[k] = split(u[:, block(k)])
            cross_zero[...] = cross_zero[...] + new[:, 4 * w :]

        def part(k, weight):
            own = weight * z[:, block(k)]
            return split(own if first else own + u[:, block(k)])

        for k in range(8):
            sums = dot3((l_high[block(n), block(k)], l_low[block(n), block(k)]), part(k, 0.5), across)
            put(half_one if k < 4 else half_zero, k % 4, sums, first)
        for c in range(4):
            p = parents[c]
            left_side = (one_high[p, block(n), :], one_low[p, block(n), :])
            right_side = part(4 + c, 1.0)
            if not first:
                zeros_c = (l_high[block(n), block(4 + c)], l_low[block(n), block(4 + c)])
                left_side = [jnp.concatenate(x, axis=0) for x in zip(left_side, (u_high[p], u_low[p]))]
                right_side = [jnp.concatenate(x, axis=0) for x in zip(right_side, zeros_c)]
            put(mixed, c, dot3(left_side, right_side, across), first)

    take_ones(OWN)
    take_zeros(OWN)
    take_band(OWN)
    to_pair(0, OWN).wait_recv()
    take_other(OWN)
    absorb(OWN, OWN, OWN)

    for step in range(1, 4):
        last = step == 3
        for chunk in (0, 2, 1):
            for way in (0, 1):
                to_ring(way, step, chunk).wait_recv()
                t = OWN - step if way == 0 else OWN + step
                if not last or (chunk == 1) == (way == 0):
                    start(to_ring(way, step + 1, chunk))
                if chunk == 0:
                    start(to_pair(0, t))
                if chunk == 2:
                    start(to_pair(1, t))
        new = (OWN - step, OWN + step)
        for t in new:
            take_ones(t)
            take_zeros(t)
            to_pair(0, t).wait_recv()
            take_other(t)
            to_pair(1, t).wait_recv()
            take_band(t)
        for t in ((), (1,), (0, 2))[step - 1]:
            take_pair(t)
        absorb(OWN - step, OWN - step + 1, OWN + step)
        absorb(OWN + step, OWN - step, OWN + step)

    far = RING - 1
    to_ring(1, 4, 0).wait_recv()
    start(to_pair(0, far))
    take_ones(far)
    to_ring(1, 4, 2).wait_recv()
    start(to_pair(1, far))
    to_ring(0, 4, 1).wait_recv()
    take_zeros(far)
    to_pair(0, far).wait_recv()
    take_other(far)
    to_pair(1, far).wait_recv()
    take_band(far)
    take_pair(OWN)
    for load in loads[3:]:
        load.wait()
    to_pair(2, 1).wait_recv()
    absorb(far, 0, far)

    for k in range(4):
        sums_one[k] = pivots_one[k] + half_one[k] + half_one[k].T
    for k in range(2):
        diag_one[k] = sums_one[2 * q + k]
        cross_one[:, block(k)] = -row_one[2 * q + k] * mask_one[k]
    stores[0].start()
    stores[1].start()
    factors = [split(factor_parent[c]) for c in range(4)]
    for c in range(4):
        p = parents[c]
        both = dot3(split(jnp.concatenate([row_one[p], sums_one[p]], axis=0)), factors[c])
        cross_zero[:, block(c)] = (both[:w] - cross_zero[:, block(c)]) * mask_zero[c]
        parent_zero[c] = mixed[c] - both[w:]
    stores[2].start()
    stores[3].start()
    for c in range(4):
        above = [jnp.concatenate(x, axis=0) for x in zip(split(mixed[c]), factors[c])]
        below = [jnp.concatenate(x, axis=0) for x in zip(factors[c], split(parent_zero[c]))]
        diag_zero[c] = pivots_zero[c] + half_zero[c] + half_zero[c].T - dot3(above, below, across)
    stores[4].start()
    for made in started:
        made.wait_send()
    for store_out in stores:
        store_out.wait()


def store(*refs):
    ins, outs, held, (load_done, store_done) = refs[:5], refs[5:10], refs[10:15], refs[15:]
    loads = [pltpu.make_async_copy(ins[n], held[n], load_done.at[n]) for n in range(5)]
    stores = [pltpu.make_async_copy(held[n], outs[n], store_done.at[n]) for n in range(5)]
    for load in loads:
        load.start()
    for load, out in zip(loads, stores):
        load.wait()
        out.start()
    for out in stores:
        out.wait()


def fused(*args):
    inverse, pivots_one, factor_one, _, pivots_zero, factor_zero, factor_parent, _, _ = args
    w = pivots_one.shape[1]
    rows = RING * w
    f32, b16 = jnp.float32, jnp.bfloat16
    vmem, smem = pl.BlockSpec(memory_space=pltpu.VMEM), pl.BlockSpec(memory_space=pltpu.SMEM)
    hbm = pl.BlockSpec(memory_space=pltpu.HBM)
    outs = (factor_one, pivots_one, factor_zero, factor_parent, pivots_zero)
    made = pl.pallas_call(
        kernel,
        out_shape=tuple(jax.ShapeDtypeStruct(x.shape, f32) for x in outs),
        in_specs=[hbm, hbm, hbm, smem, hbm, hbm, hbm, smem, smem],
        out_specs=(hbm,) * 5,
        scratch_shapes=[
            *(pltpu.VMEM(x.shape, f32) for x in outs),
            pltpu.VMEM((4, w, w), f32),
            *(pltpu.VMEM(x.shape, f32) for x in (factor_one, pivots_zero, factor_zero, factor_parent)),
            pltpu.VMEM((2, w, 4 * w), f32),
            pltpu.VMEM((RING, w, 2 * w), f32),
            pltpu.VMEM((RING, w, 2 * w), f32),
            pltpu.VMEM((RING, w, 4 * w), f32),
            pltpu.VMEM((RING, 2, w // 2 + w // 16, 4 * w), f32),
            pltpu.VMEM((rows, rows), b16),
            pltpu.VMEM((rows, rows), b16),
            pltpu.VMEM((rows, 8 * w), b16),
            pltpu.VMEM((rows, 8 * w), b16),
            pltpu.VMEM((4, rows, w), b16),
            pltpu.VMEM((4, rows, w), b16),
            pltpu.VMEM((w, 8 * w), f32),
            pltpu.VMEM((w, 8 * w), f32),
            pltpu.VMEM((4, w, w), b16),
            pltpu.VMEM((4, w, w), b16),
            *(pltpu.VMEM((4, w, w), f32) for _ in range(5)),
            pltpu.SemaphoreType.DMA((2, 4, 3)),
            pltpu.SemaphoreType.DMA((2, 4, 3)),
            pltpu.SemaphoreType.DMA((3, RING)),
            pltpu.SemaphoreType.DMA((3, RING)),
            pltpu.SemaphoreType.DMA((6,)),
            pltpu.SemaphoreType.DMA((5,)),
        ],
        compiler_params=pltpu.CompilerParams(
            collective_id=0, has_side_effects=True, vmem_limit_bytes=VMEM_BYTES
        ),
    )(*args)
    return pl.pallas_call(
        store,
        out_shape=tuple(jax.ShapeDtypeStruct(x.shape, f32) for x in outs),
        in_specs=[hbm] * 5,
        out_specs=(hbm,) * 5,
        scratch_shapes=[
            *(pltpu.VMEM(x.shape, f32) for x in outs),
            pltpu.SemaphoreType.DMA((5,)),
            pltpu.SemaphoreType.DMA((5,)),
        ],
        compiler_params=pltpu.CompilerParams(vmem_limit_bytes=VMEM_BYTES),
    )(*made)


def solution(mesh):
    in_specs = (
        P(("pole", "prow"), "pcol"),
        P(("pole", "pcol"), None, None),
        P(("pole", "prow"), "pcol"),
        P(("pole", "prow"), None),
        P(("pole", "pcol"), None, None),
        P(("pole", "prow"), "pcol"),
        P(("pole", "pcol"), None, None),
        P(("pole", "pcol")),
        P(("pole", "prow"), "pcol"),
    )
    out_specs = (
        P(("pole", "prow"), "pcol"),
        P(("pole", "pcol"), None, None),
        P(("pole", "prow"), "pcol"),
        P(("pole", "pcol"), None, None),
        P(("pole", "pcol"), None, None),
    )
    ring = (mesh.shape["prow"], mesh.shape["pcol"]) == (RING, 2)
    return jax.shard_map(fused if ring else local, mesh=mesh, in_specs=in_specs, out_specs=out_specs, check_vma=False)
```

```python
import jax
import jax.numpy as jnp
from jax import lax
from jax.experimental import pallas as pl
from jax.experimental.pallas import tpu as pltpu
from jax.sharding import PartitionSpec as P


def expand_mask(pattern, width):
    return jnp.repeat(jnp.repeat(pattern, width, 0), width, 1)


def local(
    ancestor_inverse,
    pivots_one,
    factor_one,
    pattern_one,
    pivots_zero,
    factor_zero,
    factor_parent,
    parent_index,
    pattern_zero,
):
    highest = lax.Precision.HIGHEST
    band = lax.all_gather(ancestor_inverse, "pcol", axis=1, tiled=True)
    width = pivots_one.shape[1]
    rows = band.shape[0]
    one_local = pivots_one.shape[0]
    zero_local = pivots_zero.shape[0]
    column = lax.axis_index("pcol")
    total_one = one_local * lax.axis_size("pcol")
    pattern_float = pattern_one.astype(jnp.float32)
    own_pattern = lax.dynamic_slice_in_dim(pattern_float, column * one_local, one_local, 1)
    level_one = factor_one * expand_mask(own_pattern, width)
    selector = (parent_index[:, None] == jnp.arange(total_one, dtype=jnp.int32)[None, :]).astype(
        jnp.float32
    )
    parent_pattern = jnp.dot(
        pattern_float, selector.T, precision=highest, preferred_element_type=jnp.float32
    )
    child_pattern = pattern_zero.astype(jnp.float32) * parent_pattern
    child_mask = expand_mask(child_pattern, width)
    level_zero = factor_zero * child_mask

    def add_rows(piece):
        return jnp.dot(band, piece, precision=highest, preferred_element_type=jnp.float32)

    product_one = add_rows(lax.all_gather(level_one, "prow", axis=0, tiled=True))
    product_zero = add_rows(lax.all_gather(level_zero, "prow", axis=0, tiled=True))
    cross_full = -product_one
    shaped_one = level_one.reshape(rows, one_local, width)
    diag_partial = jnp.einsum(
        "akb,akc->kbc",
        shaped_one,
        cross_full.reshape(rows, one_local, width),
        precision=highest,
        preferred_element_type=jnp.float32,
    )
    diag_sum = lax.psum(diag_partial, "prow")
    diag_one = pivots_one - diag_sum
    cross_all, diag_all = (
        lax.all_gather(cross_full, "pcol", axis=1, tiled=True),
        lax.all_gather(diag_one, "pcol", axis=0, tiled=True),
    )
    parent_cols = jnp.einsum(
        "anb,cn->acb",
        cross_all.reshape(rows, total_one, width),
        selector,
        precision=highest,
        preferred_element_type=jnp.float32,
    )
    cross_child = -product_zero.reshape(rows, zero_local, width) - jnp.einsum(
        "acb,cbd->acd",
        parent_cols,
        factor_parent,
        precision=highest,
        preferred_element_type=jnp.float32,
    )
    shaped_zero = level_zero.reshape(rows, zero_local, width)
    parent_partial = jnp.einsum(
        "acb,acd->cbd",
        parent_cols,
        shaped_zero,
        precision=highest,
        preferred_element_type=jnp.float32,
    )
    child_partial = jnp.einsum(
        "acb,acd->cbd",
        shaped_zero,
        cross_child,
        precision=highest,
        preferred_element_type=jnp.float32,
    )
    parent_sum, child_sum = lax.psum((parent_partial, child_partial), "prow")
    parents_inv = jnp.einsum(
        "cn,nbd->cbd", selector, diag_all, precision=highest, preferred_element_type=jnp.float32
    )
    parent_zero = -parent_sum - jnp.einsum(
        "cbe,ced->cbd",
        parents_inv,
        factor_parent,
        precision=highest,
        preferred_element_type=jnp.float32,
    )
    diag_zero = (
        pivots_zero
        - child_sum
        - jnp.einsum(
            "cba,cbd->cad",
            factor_parent,
            parent_zero,
            precision=highest,
            preferred_element_type=jnp.float32,
        )
    )
    cross_one = cross_full * expand_mask(own_pattern, width)
    cross_zero = cross_child.reshape(rows, zero_local * width) * child_mask
    return (cross_one, diag_one, cross_zero, parent_zero, diag_zero)


VMEM_BYTES = 64 * 1024 * 1024
RING = 8
OWN = 3
HALF = 5


def split(x):
    high = x.astype(jnp.bfloat16)
    return high, (x - high.astype(jnp.float32)).astype(jnp.bfloat16)


def dot3(a, b, dims=((1,), (0,))):
    def one(x, y):
        return lax.dot_general(x, y, (dims, ((), ())), preferred_element_type=jnp.float32)

    return one(a[0], b[0]) + (one(a[0], b[1]) + one(a[1], b[0]))


def natural(place):
    return 2 * place + (place // 4) * (15 - 4 * place)


def kernel(
    inverse, pivots_one_hbm, factor_one_hbm, pattern_one, pivots_zero_hbm, factor_zero_hbm, factor_parent_hbm,
    parent, pattern_zero, cross_one_hbm, diag_one_hbm, cross_zero_hbm, parent_zero_hbm, diag_zero_hbm,
    cross_one, diag_one, cross_zero, parent_zero, diag_zero, pivots_one, factor_one, pivots_zero, factor_zero, factor_parent, row, ones, ones_other, zeros, band, a_high, a_low, l_high, l_low, one_high, one_low,
    z, u, u_high, u_low, half_one, half_zero, mixed, row_one, sums_one,
    ring_send, ring_recv, pair_send, pair_recv, load_done, store_done,
):
    w = pivots_zero.shape[1]
    half_row, eighth = w // 2, w // 16
    pole, prow, q = lax.axis_index("pole"), lax.axis_index("prow"), lax.axis_index("pcol")
    z_at, x_at = prow // 2, prow % 2
    place = z_at + x_at * (RING - 1 - 2 * z_at)
    right = (pole, natural((place + 1) % RING), q)
    left = (pole, natural((place + RING - 1) % RING), q)
    other = (pole, prow, 1 - q)

    barrier = pltpu.get_barrier_semaphore()
    for peer in (left, right, other):
        pl.semaphore_signal(barrier, inc=1, device_id=peer, device_id_type=pl.DeviceIdType.MESH)

    loads = [
        pltpu.make_async_copy(src, dst, load_done.at[n])
        for n, (src, dst) in enumerate(
            (
                (factor_one_hbm, factor_one),
                (factor_zero_hbm, factor_zero),
                (inverse, row.at[q]),
                (pivots_one_hbm, pivots_one.at[pl.ds(2 * q, 2)]),
                (pivots_zero_hbm, pivots_zero),
                (factor_parent_hbm, factor_parent),
            )
        )
    ]
    for load in loads:
        load.start()

    def block(k):
        return slice(k * w, (k + 1) * w)

    def flag(value):
        return value.astype(jnp.float32)

    mask_one = [flag(pattern_one[0, 2 * q + k]) for k in range(2)]
    parents = [parent[c] for c in range(4)]
    parent_mask = [sum(flag(p == k) * flag(pattern_one[0, k]) for k in range(4)) for p in parents]
    mask_zero = [flag(pattern_zero[0, c]) * parent_mask[c] for c in range(4)]
    loads[0].wait()
    for k in range(2):
        ones[OWN, :, block(k)] = factor_one[:, block(k)] * mask_one[k]
    loads[1].wait()
    for c in range(4):
        zeros[OWN, :, block(c)] = factor_zero[:, block(c)] * mask_zero[c]

    def copy(src, dst, send, recv, peer):
        return pltpu.make_async_remote_copy(
            src_ref=src, dst_ref=dst, send_sem=send, recv_sem=recv,
            device_id=peer, device_id_type=pl.DeviceIdType.MESH,
        )

    def to_ring(way, step, chunk):
        sign = -1 if way == 0 else 1
        source, target = OWN + sign * (step - 1), (OWN + sign * step) % RING
        ref = (ones, zeros, band)[chunk]
        src, dst = ref.at[source], ref.at[target]
        if chunk == 2:
            src, dst = ref.at[source, q], ref.at[target, q]
        place_at = (way, step - 1, chunk)
        return copy(src, dst, ring_send.at[place_at], ring_recv.at[place_at], right if way == 0 else left)

    def to_pair(kind, slot):
        if kind == 0:
            src, dst = ones.at[slot], ones_other.at[slot]
        elif kind == 1:
            src, dst = band.at[slot, q], band.at[slot, q]
        elif slot == 0:
            src, dst = inverse, row.at[q]
        else:
            src, dst = pivots_one_hbm, pivots_one.at[pl.ds(2 * q, 2)]
        return copy(src, dst, pair_send.at[kind, slot], pair_recv.at[kind, slot], other)

    stores = [
        pltpu.make_async_copy(src, dst, store_done.at[n])
        for n, (src, dst) in enumerate(
            (
                (cross_one, cross_one_hbm),
                (diag_one, diag_one_hbm),
                (cross_zero, cross_zero_hbm),
                (parent_zero, parent_zero_hbm),
                (diag_zero, diag_zero_hbm),
            )
        )
    ]
    started = []

    def start(made):
        made.start()
        started.append(made)

    pl.semaphore_wait(barrier, 3)
    start(to_pair(2, 0))
    for way in (0, 1):
        start(to_ring(way, 1, 0))
    start(to_pair(0, OWN))
    start(to_pair(2, 1))

    loads[2].wait()
    to_pair(2, 0).wait_recv()
    for d in range(HALF):
        column = natural((place + d) % RING)
        source = (column // 4, slice(None), pl.ds(pl.multiple_of((column % 4) * w, w), w))
        piece = row[source]
        for h in range(2):
            if d < HALF - 1:
                band[OWN, h, :half_row, block(d)] = piece[h * half_row : (h + 1) * half_row]
            else:
                sent = jnp.where(place < RING // 2, piece[:half_row], piece.T[half_row:])
                for n in range(4):
                    at = (4 * h + n) * eighth
                    band[OWN, h, half_row:, block(n)] = sent[at : at + eighth]
    for chunk in (2, 1):
        for way in (0, 1):
            start(to_ring(way, 1, chunk))

    def take_band(t):
        for d in range(HALF - 1):
            piece = jnp.concatenate([band[t, h, :half_row, block(d)] for h in range(2)], axis=0)
            u = (t + d) % RING
            a_high[block(t), block(u)], a_low[block(t), block(u)] = split(piece)
            if d > 0:
                a_high[block(u), block(t)], a_low[block(u), block(t)] = split(piece.T)

    def take_pair(t):
        u = t + RING // 2
        low = (place + t + RING - OWN) % RING < RING // 2
        at_t, at_u = (
            jnp.concatenate([band[v, h, half_row:, block(n)] for h in range(2) for n in range(4)], axis=0)
            for v in (t, u)
        )
        piece = jnp.concatenate([jnp.where(low, at_t, at_u), jnp.where(low, at_u, at_t)], axis=0)
        turned = piece.T
        a_high[block(t), block(u)], a_low[block(t), block(u)] = split(jnp.where(low, piece, turned))
        a_high[block(u), block(t)], a_low[block(u), block(t)] = split(jnp.where(low, turned, piece))

    def take_half(t, blocks, column):
        high, low = split(blocks[t])
        lanes = pl.ds(pl.multiple_of(2 * column * w, 2 * w), 2 * w)
        l_high[block(t), lanes], l_low[block(t), lanes] = high, low
        for k in range(2):
            one_high[2 * column + k, block(t), :] = high[:, block(k)]
            one_low[2 * column + k, block(t), :] = low[:, block(k)]

    def take_ones(t):
        take_half(t, ones, q)

    def take_other(t):
        take_half(t, ones_other, 1 - q)

    def take_zeros(t):
        l_high[block(t), 4 * w :], l_low[block(t), 4 * w :] = split(zeros[t])

    def times(n, lo, hi):
        inner = slice(lo * w, hi * w)
        return dot3((a_high[block(n), inner], a_low[block(n), inner]), (l_high[inner, :], l_low[inner, :]))

    across = ((0,), (0,))

    def put(ref, k, value, first):
        ref[k] = value if first else ref[k] + value

    def absorb(n, lo, hi):
        first = lo == hi
        z[...] = times(n, n, n + 1)
        if first:
            for k in range(4):
                row_one[k] = z[:, block(k)]
            cross_zero[...] = z[:, 4 * w :]
        else:
            u[...] = times(n, lo, hi)
            new = times(OWN, n, n + 1)
            for k in range(4):
                row_one[k] = row_one[k] + new[:, block(k)]
                u_high[k], u_low[k] = split(u[:, block(k)])
            cross_zero[...] = cross_zero[...] + new[:, 4 * w :]

        def part(k, weight):
            own = weight * z[:, block(k)]
            return split(own if first else own + u[:, block(k)])

        for k in range(8):
            sums = dot3((l_high[block(n), block(k)], l_low[block(n), block(k)]), part(k, 0.5), across)
            put(half_one if k < 4 else half_zero, k % 4, sums, first)
        for c in range(4):
            p = parents[c]
            left_side = (one_high[p, block(n), :], one_low[p, block(n), :])
            right_side = part(4 + c, 1.0)
            if not first:
                zeros_c = (l_high[block(n), block(4 + c)], l_low[block(n), block(4 + c)])
                left_side = [jnp.concatenate(x, axis=0) for x in zip(left_side, (u_high[p], u_low[p]))]
                right_side = [jnp.concatenate(x, axis=0) for x in zip(right_side, zeros_c)]
            put(mixed, c, dot3(left_side, right_side, across), first)

    take_ones(OWN)
    take_zeros(OWN)
    take_band(OWN)
    to_pair(0, OWN).wait_recv()
    take_other(OWN)
    absorb(OWN, OWN, OWN)

    for step in range(1, 4):
        last = step == 3
        for chunk in (0, 2, 1) if step == 1 else (2, 0, 1):
            for way in (0, 1):
                to_ring(way, step, chunk).wait_recv()
                t = OWN - step if way == 0 else OWN + step
                if chunk == 0:
                    start(to_pair(0, t))
                if chunk == 2:
                    start(to_pair(1, t))
                if not (step == 1 and chunk == 0) and (not last or (chunk == 1) == (way == 0)):
                    start(to_ring(way, step + 1, chunk))
            if step == 1 and chunk == 2:
                for way in (0, 1):
                    start(to_ring(way, 2, 0))
        new = (OWN - step, OWN + step)
        for t in new:
            take_ones(t)
            take_zeros(t)
            to_pair(0, t).wait_recv()
            take_other(t)
            to_pair(1, t).wait_recv()
            take_band(t)
        for t in ((), (1,), (0, 2))[step - 1]:
            take_pair(t)
        absorb(OWN - step, OWN - step + 1, OWN + step)
        absorb(OWN + step, OWN - step, OWN + step)

    far = RING - 1
    to_ring(1, 4, 2).wait_recv()
    start(to_pair(1, far))
    to_pair(1, far).wait_recv()
    take_band(far)
    take_pair(OWN)
    to_ring(1, 4, 0).wait_recv()
    start(to_pair(0, far))
    take_ones(far)
    to_ring(0, 4, 1).wait_recv()
    take_zeros(far)
    to_pair(0, far).wait_recv()
    take_other(far)
    for load in loads[3:]:
        load.wait()
    to_pair(2, 1).wait_recv()
    absorb(far, 0, far)

    for k in range(4):
        sums_one[k] = pivots_one[k] + half_one[k] + half_one[k].T
    for k in range(2):
        diag_one[k] = sums_one[2 * q + k]
        cross_one[:, block(k)] = -row_one[2 * q + k] * mask_one[k]
    stores[0].start()
    stores[1].start()
    factors = [split(factor_parent[c]) for c in range(4)]
    for c in range(4):
        p = parents[c]
        both = dot3(split(jnp.concatenate([row_one[p], sums_one[p]], axis=0)), factors[c])
        cross_zero[:, block(c)] = (both[:w] - cross_zero[:, block(c)]) * mask_zero[c]
        parent_zero[c] = mixed[c] - both[w:]
    stores[2].start()
    stores[3].start()
    for c in range(4):
        above = [jnp.concatenate(x, axis=0) for x in zip(split(mixed[c]), factors[c])]
        below = [jnp.concatenate(x, axis=0) for x in zip(factors[c], split(parent_zero[c]))]
        diag_zero[c] = pivots_zero[c] + half_zero[c] + half_zero[c].T - dot3(above, below, across)
    stores[4].start()
    for made in started:
        made.wait_send()
    for store_out in stores:
        store_out.wait()


def store(*refs):
    ins, outs, held, (load_done, store_done) = refs[:5], refs[5:10], refs[10:15], refs[15:]
    loads = [pltpu.make_async_copy(ins[n], held[n], load_done.at[n]) for n in range(5)]
    stores = [pltpu.make_async_copy(held[n], outs[n], store_done.at[n]) for n in range(5)]
    for load in loads:
        load.start()
    for load, out in zip(loads, stores):
        load.wait()
        out.start()
    for out in stores:
        out.wait()


def fused(*args):
    inverse, pivots_one, factor_one, _, pivots_zero, factor_zero, factor_parent, _, _ = args
    w = pivots_one.shape[1]
    rows = RING * w
    f32, b16 = jnp.float32, jnp.bfloat16
    vmem, smem = pl.BlockSpec(memory_space=pltpu.VMEM), pl.BlockSpec(memory_space=pltpu.SMEM)
    hbm = pl.BlockSpec(memory_space=pltpu.HBM)
    outs = (factor_one, pivots_one, factor_zero, factor_parent, pivots_zero)
    made = pl.pallas_call(
        kernel,
        out_shape=tuple(jax.ShapeDtypeStruct(x.shape, f32) for x in outs),
        in_specs=[hbm, hbm, hbm, smem, hbm, hbm, hbm, smem, smem],
        out_specs=(hbm,) * 5,
        scratch_shapes=[
            *(pltpu.VMEM(x.shape, f32) for x in outs),
            pltpu.VMEM((4, w, w), f32),
            *(pltpu.VMEM(x.shape, f32) for x in (factor_one, pivots_zero, factor_zero, factor_parent)),
            pltpu.VMEM((2, w, 4 * w), f32),
            pltpu.VMEM((RING, w, 2 * w), f32),
            pltpu.VMEM((RING, w, 2 * w), f32),
            pltpu.VMEM((RING, w, 4 * w), f32),
            pltpu.VMEM((RING, 2, w // 2 + w // 16, 4 * w), f32),
            pltpu.VMEM((rows, rows), b16),
            pltpu.VMEM((rows, rows), b16),
            pltpu.VMEM((rows, 8 * w), b16),
            pltpu.VMEM((rows, 8 * w), b16),
            pltpu.VMEM((4, rows, w), b16),
            pltpu.VMEM((4, rows, w), b16),
            pltpu.VMEM((w, 8 * w), f32),
            pltpu.VMEM((w, 8 * w), f32),
            pltpu.VMEM((4, w, w), b16),
            pltpu.VMEM((4, w, w), b16),
            *(pltpu.VMEM((4, w, w), f32) for _ in range(5)),
            pltpu.SemaphoreType.DMA((2, 4, 3)),
            pltpu.SemaphoreType.DMA((2, 4, 3)),
            pltpu.SemaphoreType.DMA((3, RING)),
            pltpu.SemaphoreType.DMA((3, RING)),
            pltpu.SemaphoreType.DMA((6,)),
            pltpu.SemaphoreType.DMA((5,)),
        ],
        compiler_params=pltpu.CompilerParams(
            collective_id=0, has_side_effects=True, vmem_limit_bytes=VMEM_BYTES
        ),
    )(*args)
    return pl.pallas_call(
        store,
        out_shape=tuple(jax.ShapeDtypeStruct(x.shape, f32) for x in outs),
        in_specs=[hbm] * 5,
        out_specs=(hbm,) * 5,
        scratch_shapes=[
            *(pltpu.VMEM(x.shape, f32) for x in outs),
            pltpu.SemaphoreType.DMA((5,)),
            pltpu.SemaphoreType.DMA((5,)),
        ],
        compiler_params=pltpu.CompilerParams(vmem_limit_bytes=VMEM_BYTES),
    )(*made)


def solution(mesh):
    in_specs = (
        P(("pole", "prow"), "pcol"),
        P(("pole", "pcol"), None, None),
        P(("pole", "prow"), "pcol"),
        P(("pole", "prow"), None),
        P(("pole", "pcol"), None, None),
        P(("pole", "prow"), "pcol"),
        P(("pole", "pcol"), None, None),
        P(("pole", "pcol")),
        P(("pole", "prow"), "pcol"),
    )
    out_specs = (
        P(("pole", "prow"), "pcol"),
        P(("pole", "pcol"), None, None),
        P(("pole", "prow"), "pcol"),
        P(("pole", "pcol"), None, None),
        P(("pole", "pcol"), None, None),
    )
    ring = (mesh.shape["prow"], mesh.shape["pcol"]) == (RING, 2)
    return jax.shard_map(fused if ring else local, mesh=mesh, in_specs=in_specs, out_specs=out_specs, check_vma=False)
```
